128 devices in a mesh: tm: 32 (over y, x, core), zone: 4 (over z).
Axes of the slice: x: 4, y: 4, z: 4, core: 2. Of those that a mesh axis runs over, the one named last changes fastest.
Arguments:
- gains: float32 [8192, 128, 128], P(('tm', 'zone')), may hold values from -1 to 1, as said below
- means: float32 [8192, 128], P(('tm', 'zone')), may hold values from -0.4 to 0.4
- transition: float32 [128, 128], replicated, may hold values from -0.25 to 0.25
- observations: bfloat16 [8192, 98304], P('tm', 'zone'), may hold values from -6 to 6
- loadings: bfloat16 [98304, 128], P('zone'), may hold values from -0.5 to 0.5
Outputs:
- smoothed: float32 [8192, 128], P(('tm', 'zone'))
- load_grad: float32 [98304, 128], P(('zone', 'tm'))
The draws below stay inside these ranges and needn't reach their ends.
Inputs may be any that keep to these rules, and one draw needn't show every extreme that they name: `gains`: one 128 x 128 gain matrix a time step.
All inputs are finite; a program needn't handle non-finite values.
Results may differ from the reference program's by a relative error of at most 0.0009.
Values may be sent and summed in bfloat16 or wider, within the bound.
No kernel may reach another device: no remote copies, remote signals or barrier semaphores. Data moves between devices by JAX's collectives and lax.ppermute only.
A program may use at most 192 MiB of HBM per device.

```python
import jax
import jax.numpy as jnp
from jax import lax

K = 128
ZONES = 98304
TIME = 8192
N_TM = 32
N_ZONE = 4


def draw_gains(key, part):
    key = jax.random.fold_in(key, 5)
    key_a, key_b, key_c, key_d, key_e, key_f = jax.random.split(key, 6)
    share = 0.5
    noise = jnp.clip(jax.random.normal(key_c, (TIME, K, K), jnp.float32), -4.0, 4.0)
    slow = jax.random.uniform(key_a, (K,), jnp.float32) < share
    keep = jax.random.uniform(key_b, (K,), jnp.float32, 0.1, 0.5)
    slow_rate = jnp.exp(jnp.log(keep) / TIME)
    span = jax.random.uniform(key_f, (K,), jnp.float32, 30.0, 50.0)
    fast_rate = jnp.exp(-1.0 / span)
    rate = jnp.where(slow, slow_rate, fast_rate)
    diag_gain = jnp.sqrt(jnp.maximum(rate * rate - 0.04 * share, 0.5))
    spots = jax.random.randint(key_d, (4,), 0, TIME)
    steps = jnp.arange(TIME)
    struck = jnp.any(steps[:, None] == spots[None, :], axis=1)
    cut = jax.random.uniform(key_e, (TIME, K), jnp.float32, 0.5, 0.8)
    diag_all = diag_gain[None, :] * jnp.where(struck[:, None], cut, 1.0)
    eye = jnp.eye(K, dtype=jnp.float32)
    off_part = noise * (0.2 / jnp.sqrt(1.0 * K)) * (1.0 - eye)
    return off_part + diag_all[:, :, None] * eye[None, :, :]


def spiked(array, key, source, target, blocks, factor):
    def block_of(position):
        return (jnp.arange(array.shape[position]) // (array.shape[position] // blocks)).reshape((-1,) + (1,) * (array.ndim - 1 - position))

    near = jax.random.permutation(key, blocks)[block_of(target)]
    second = (block_of(target) + blocks // 2) % blocks
    return jnp.where((block_of(source) == near) | (block_of(source) == second), factor * array, array)


def block_scale(rng, dims, pieces, least, high):
    loudness = 1.0
    for axis_at, parts in pieces:
        draws = jax.random.uniform(jax.random.fold_in(jax.random.fold_in(rng, 6), axis_at), (parts,), jnp.float32, least / len(pieces), high / len(pieces))
        loudness = loudness * jnp.repeat(jnp.exp(draws), dims[axis_at] // parts).reshape((-1,) + (1,) * (len(dims) - 1 - axis_at))
    return loudness


def normal_values(rng, shape, scale, most, pieces=(), kind=jnp.bfloat16):
    result = jax.random.normal(rng, shape, jnp.float32) * scale
    if len(pieces) > 0:
        result = block_scale(rng, shape, pieces, -0.22, 0.18) * result
    return jnp.clip(result, min=-most, max=most).astype(kind)


def bell_draw_with(stream_key, shape, scale, reach, cuts, heavy, held_as=jnp.bfloat16):
    result = scale * jax.random.normal(stream_key, shape, jnp.float32)
    if cuts:
        result = result * block_scale(stream_key, shape, cuts, -0.22, 0.18)
    return jnp.clip(spiked(result, jax.random.fold_in(stream_key, 3), *heavy), -reach, reach).astype(held_as)


def setup_inputs(seed: int = 0) -> dict:
    streams_of = jax.random.split(jax.random.key(seed), 6)
    return {
        "gains": draw_gains(jax.random.fold_in(streams_of[5], 71), 0),
        "means": normal_values(streams_of[1], (TIME, K), 0.05, 0.4, ((0, 128),), jnp.float32),
        "transition": normal_values(streams_of[2], (K, K), (4 * K) ** -0.5, 0.25, (), jnp.float32),
        "observations": bell_draw_with(streams_of[3], (TIME, ZONES), 1.0, 6.0, ((0, 32), (1, 4)), (0, 1, 32, 2.75)),
        "loadings": normal_values(streams_of[4], (ZONES, K), K ** -0.5, 0.5, ((0, 4),)),
    }


def reference(gains, means, transition, observations, loadings):
    highest = lax.Precision.HIGHEST
    predicted = jnp.dot(means, transition.T, precision=highest)
    offsets = means - jnp.einsum('tij,tj->ti', gains, predicted, precision=highest)
    begin_state = predicted[-1]

    def advance(state, item):
        gain, offset = item
        fresh = jnp.dot(gain, state, precision=highest) + offset
        return fresh, fresh

    _, smoothed = lax.scan(advance, begin_state, (gains, offsets), reverse=True)
    states = smoothed.astype(jnp.bfloat16)
    width = ZONES // (N_TM * N_ZONE)

    def block_term(number):
        first = (number * width).astype(jnp.int32)
        rows = lax.dynamic_slice_in_dim(loadings, first, width, 0)
        cols = lax.dynamic_slice_in_dim(observations, first, width, 1)
        fitted = jnp.dot(states, rows.T, preferred_element_type=jnp.float32)
        resid = (fitted - cols.astype(jnp.float32)).astype(jnp.bfloat16)
        return lax.dot_general(resid, states, (((0,), (0,)), ((), ())), preferred_element_type=jnp.float32)

    terms = lax.map(block_term, jnp.arange(N_TM * N_ZONE, dtype=jnp.int32))
    load_grad = terms.reshape(ZONES, K) / TIME
    return smoothed, load_grad
```

```python
import jax
import jax.numpy as jnp
from jax import lax
from jax.experimental import pallas as pl
from jax.experimental.pallas import tpu as pltpu
from jax.sharding import PartitionSpec as P

K = 128
AUG = 136
CHUNK = 8
SIDE = 4
HALF = 384
TM = (4, 4, 2)
Y, X, CORE = 0, 1, 2
HIGH = lax.Precision.HIGHEST
F32 = jnp.float32
BF16 = jnp.bfloat16
NT = (((1,), (1,)), ((), ()))
NN = (((1,), (0,)), ((), ()))
VM = pl.BlockSpec(memory_space=pltpu.VMEM)
SM = pl.BlockSpec(memory_space=pltpu.SMEM)
HBM = pl.BlockSpec(memory_space=pltpu.HBM)


def params(mib):
    return pltpu.CompilerParams(vmem_limit_bytes=mib << 20)


def thirds(x):
    a = x.astype(BF16)
    x = x - a.astype(F32)
    b = x.astype(BF16)
    return a, b, (x - b.astype(F32)).astype(BF16)


def dot32(a, b, dims):
    a0, a1, a2 = thirds(a)
    b0, b1, b2 = thirds(b)
    at = dims[0][1][0]

    def two(p, q):
        left, right = jnp.concatenate(p, axis=1), jnp.concatenate(q, axis=at)
        return lax.dot_general(left, right, dims, preferred_element_type=F32)

    return two((a0, a1), (b0, b0)) + (two((a0, a1), (b1, b1)) + two((a0, a2), (b2, b0)))


def first_row(row):
    at = lax.broadcasted_iota(jnp.int32, (8, K), 0)
    return jnp.where(at == 0, jnp.broadcast_to(row, (8, K)), 0.0)


def identity_map():
    at = lax.broadcasted_iota(jnp.int32, (AUG, K), 0)
    to = lax.broadcasted_iota(jnp.int32, (AUG, K), 1)
    return jnp.where(at == to, 1.0, 0.0).astype(F32)


def then(late, early):
    out = dot32(late, early[:K], NN)
    return out + jnp.concatenate([jnp.zeros((K, K), F32), early[K:]], axis=0)


def local_kernel(at_ref, gains, obs, means, transition, maps, tails, shifted, whole, theirs, g, buf, gsem, isem, osem):
    chunks = gains.shape[0]
    steps = chunks * CHUNK
    width = 2 * HALF
    blocks = buf.shape[0]

    def gain_copy(s):
        return pltpu.make_async_copy(gains.at[:, s], g.at[s], gsem.at[s])

    def obs_in(b):
        col = pl.multiple_of((2 * b + 1 - at_ref[1]) * width, width)
        return pltpu.make_async_copy(obs.at[:, pl.ds(col, width)], buf.at[b], isem.at[b])

    def obs_out(b):
        col = pl.multiple_of(b * width, width)
        return pltpu.make_async_copy(buf.at[b], theirs.at[:, pl.ds(col, width)], osem.at[b])

    for s in range(CHUNK - 1, -1, -1):
        gain_copy(s).start()
    for b in range(blocks):
        obs_in(b).start()

    m = means[...]
    p = lax.dot_general(m, transition[...], NT, precision=HIGH, preferred_element_type=F32)
    sh = jnp.concatenate([jnp.zeros((1, K), F32), p[: steps - 1]], axis=0)
    shifted[...] = sh
    whole[0:steps, :] = m - sh
    enter = jnp.where(at_ref[0] == 1, 0.0, -p[steps - 1 : steps])

    gain_copy(CHUNK - 1).wait()
    for c in range(chunks):
        t = CHUNK * c + CHUNK - 1
        gain = g[CHUNK - 1, c]
        maps[t, 0:K, :] = gain.T
        row = first_row(whole[t : t + 1, :])
        if c == chunks - 1:
            row = row + dot32(first_row(enter), gain, NT)
        maps[t, K:AUG, :] = row

    def step(i, _):
        s = CHUNK - 2 - i
        gain_copy(s).wait()
        late = [maps[CHUNK * c + s + 1] for c in range(chunks)]
        gain = [g[s, c] for c in range(chunks)]
        out = [dot32(late[c], gain[c], NT) for c in range(chunks)]
        rows = [first_row(whole[pl.ds(CHUNK * c + s, 1), :]) for c in range(chunks)]
        for c in range(chunks):
            maps[CHUNK * c + s, 0:K, :] = out[c][:K]
            maps[CHUNK * c + s, K:AUG, :] = out[c][K:] + rows[c]
        for b in (2 * i, 2 * i + 1):
            obs_in(b).wait()
            obs_out(b).start()
        return 0

    lax.fori_loop(0, CHUNK - 1, step, 0)
    for b in range(2 * (CHUNK - 1), blocks):
        obs_in(b).wait()
        obs_out(b).start()
    run = maps[CHUNK * (chunks - 1)]
    tails[chunks - 1] = run
    for c in range(chunks - 2, -1, -1):
        run = then(run, maps[CHUNK * c])
        tails[c] = run
    whole[...] = run
    for b in range(blocks):
        obs_out(b).wait()


def local_maps(places, gains, obs, means, transition):
    steps = gains.shape[0]
    chunks = steps // CHUNK
    rows, cols = obs.shape
    blocks = cols // (4 * HALF)
    return pl.pallas_call(
        local_kernel,
        out_shape=(
            jax.ShapeDtypeStruct((steps, AUG, K), F32),
            jax.ShapeDtypeStruct((chunks, AUG, K), F32),
            jax.ShapeDtypeStruct((steps, K), F32),
            jax.ShapeDtypeStruct((AUG, K), F32),
            jax.ShapeDtypeStruct((rows, cols // 2), obs.dtype),
        ),
        in_specs=[SM, HBM, HBM, VM, VM],
        out_specs=(VM, VM, VM, VM, HBM),
        scratch_shapes=[
            pltpu.VMEM((CHUNK, chunks, K, K), F32),
            pltpu.VMEM((blocks, rows, 2 * HALF), obs.dtype),
            pltpu.SemaphoreType.DMA((CHUNK,)),
            pltpu.SemaphoreType.DMA((blocks,)),
            pltpu.SemaphoreType.DMA((blocks,)),
        ],
        compiler_params=params(57),
    )(places, gains.reshape(chunks, CHUNK, K, K), obs, means, transition)


def pick(refs, offset, count):
    offset = lax.rem(offset + count, count)
    out = refs[0][...]
    for i in range(1, count):
        out = jnp.where(offset == i, refs[i][...], out)
    return out


def four_kernel(place_ref, *refs):
    ins, (after, total) = refs[:SIDE], refs[SIDE:]
    place = place_ref[0]
    w = [pick(ins, other - place, SIDE) for other in range(SIDE)]
    late, early = then(w[3], w[2]), then(w[1], w[0])
    total[...] = then(late, early)
    middle = then(late, w[1])
    tail = jnp.where(place == 3, identity_map(), w[3])
    tail = jnp.where(place == 1, late, tail)
    after[...] = jnp.where(place == 0, middle, tail)


def pair_kernel(place_ref, mine, theirs, after, total):
    first = place_ref[0] == 0
    late = jnp.where(first, theirs[...], mine[...])
    early = jnp.where(first, mine[...], theirs[...])
    after[...] = jnp.where(first, late, identity_map())
    total[...] = then(late, early)


def group_maps(kernel, place, parts):
    one = jax.ShapeDtypeStruct((AUG, K), F32)
    return pl.pallas_call(
        kernel,
        out_shape=(one, one),
        in_specs=[SM] + [VM] * len(parts),
        out_specs=(VM, VM),
        compiler_params=params(4),
    )(place, *parts)


def apply_map(row, m):
    col = jnp.broadcast_to(row, (K, K)).T
    return jnp.sum(col * m[:K], axis=0, keepdims=True) + m[K : K + 1]


def final_kernel(place_ref, *refs):
    ins = refs[:SIDE]
    by_x, by_core, by_z, tails, maps, shifted, smoothed, states = refs[SIDE:]
    steps = maps.shape[0]
    chunks = steps // CHUNK
    place = place_ref[0]
    v = jnp.zeros((1, K), F32)
    for other in range(SIDE - 1, 0, -1):
        v = jnp.where(other > place, apply_map(v, pick(ins, other - place, SIDE)), v)
    v = apply_map(v, by_x[...])
    v = apply_map(v, by_core[...])
    v = apply_map(v, by_z[...])
    col = jnp.broadcast_to(v, (K, K)).T
    for c in range(chunks):
        if c == chunks - 1:
            enter = col
        else:
            m = tails[c + 1]
            enter = jnp.sum(col * m[:K], axis=0, keepdims=True) + m[K : K + 1]
            enter = jnp.broadcast_to(enter, (K, K)).T
        rows = []
        for s in range(CHUNK):
            t = CHUNK * c + s
            rows.append(jnp.sum(enter * maps[t, 0:K, :], axis=0, keepdims=True) + maps[t, K : K + 1, :])
        out = jnp.concatenate(rows, axis=0) + shifted[CHUNK * c : CHUNK * (c + 1), :]
        smoothed[CHUNK * c : CHUNK * (c + 1), :] = out
    states[...] = smoothed[...].astype(BF16)


def final_states(place, parts, by_x, by_core, by_z, tails, maps, shifted):
    shape = shifted.shape
    return pl.pallas_call(
        final_kernel,
        out_shape=(jax.ShapeDtypeStruct(shape, F32), jax.ShapeDtypeStruct(shape, BF16)),
        in_specs=[SM] + [VM] * (SIDE + 6),
        out_specs=(VM, VM),
        compiler_params=params(4),
    )(place, *parts, by_x, by_core, by_z, tails, maps, shifted)


def routes(sizes, dim, hop_of):
    stride, total = 1, 1
    for s in sizes[dim + 1 :]:
        stride *= s
    for s in sizes:
        total *= s
    pairs = []
    for at in range(total):
        mine = (at // stride) % sizes[dim]
        pairs.append((at, at + ((mine + hop_of(at)) % sizes[dim] - mine) * stride))
    return pairs


def from_later(value, axis, sizes, dim):
    got = [value]
    for hop in range(1, sizes[dim]):
        got.append(lax.ppermute(value, axis, routes(sizes, dim, lambda _: -hop)))
    return got


def stat_kernel(groups, adding, at_ref, *refs):
    units = groups * SIDE
    parts, (obs_own, obs_far, load), refs = refs[:SIDE], refs[SIDE : SIDE + 3], refs[SIDE + 3 :]
    adds, refs = refs[:adding], refs[adding:]
    outs, (obs, rows_of, states, sems) = refs[:groups], refs[groups:]
    rows = parts[0].shape[1]
    span = SIDE * rows

    def copies(i):
        own = pl.multiple_of(at_ref[i] * HALF, HALF)
        far = pl.multiple_of(at_ref[units + i] * HALF, HALF)
        return (
            pltpu.make_async_copy(obs_own.at[:, pl.ds(own, HALF)], obs.at[i, pl.ds(0, span)], sems.at[i, 0]),
            pltpu.make_async_copy(obs_far.at[:, pl.ds(far, HALF)], obs.at[i, pl.ds(span, span)], sems.at[i, 1]),
            pltpu.make_async_copy(load.at[pl.ds(own, HALF)], rows_of.at[i], sems.at[i, 2]),
        )

    for i in range(units):
        for copy in copies(i):
            copy.start()
    for hop in range(SIDE):
        at = lax.rem(at_ref[2 * units] + hop, SIDE) * rows
        for side in range(2):
            states[pl.ds(pl.multiple_of(at + side * span, rows), rows), :] = parts[hop][side]

    for g in range(groups):

        def unit(u, _, g=g):
            i = SIDE * g + u
            for copy in copies(i):
                copy.wait()
            fitted = lax.dot_general(rows_of[i], states[...], NT, preferred_element_type=F32)
            resid = (fitted - obs[i].T.astype(F32)).astype(BF16)
            term = jnp.dot(resid, states[...], preferred_element_type=F32)
            if g < adding:
                term = term + adds[g][u]
            outs[g][u] = term
            return 0

        lax.fori_loop(0, SIDE, unit, 0)


def stat_units(units, adds, z, parts, obs_own, obs_far, load):
    groups = len(units)
    n = groups * SIDE
    at = jnp.concatenate([u[0] for u in units] + [u[1] for u in units] + [z])
    rows = obs_own.shape[0]
    flops = n * HALF * rows * 2 * K * 4
    moved = n * HALF * (rows * 4 + K * 6)
    return pl.pallas_call(
        lambda *refs: stat_kernel(groups, len(adds), *refs),
        out_shape=[jax.ShapeDtypeStruct((SIDE, HALF, K), F32)] * groups,
        in_specs=[SM] + [VM] * SIDE + [HBM] * 3 + [VM] * len(adds),
        out_specs=[VM] * groups,
        scratch_shapes=[
            pltpu.VMEM((n, 2 * rows, HALF), BF16),
            pltpu.VMEM((n, HALF, K), BF16),
            pltpu.VMEM((2 * rows, K), BF16),
            pltpu.SemaphoreType.DMA((n, 3)),
        ],
        cost_estimate=pl.CostEstimate(flops=flops, bytes_accessed=moved, transcendentals=0),
        compiler_params=params(58),
    )(at, *parts, obs_own, obs_far, load, *adds)


def join_kernel(at_ref, *refs):
    ins, outs = refs[:6], refs[6:]
    for side in range(2):
        a, b, c = ins[3 * side : 3 * side + 3]
        for j in range(SIDE):
            d = at_ref[j]
            outs[SIDE * side + j][...] = a[d] + b[d] + c[d]


def join_units(order, parts):
    return pl.pallas_call(
        join_kernel,
        out_shape=[jax.ShapeDtypeStruct((HALF, K), F32)] * (2 * SIDE),
        in_specs=[SM] + [VM] * 6,
        out_specs=[VM] * (2 * SIDE),
        compiler_params=params(4),
    )(order, *parts)


def add_kernel(a, b, c, d, e, f):
    e[...] = a[...] + b[...]
    f[...] = c[...] + d[...]


def add_two(a, b, c, d):
    return pl.pallas_call(
        add_kernel,
        out_shape=[jax.ShapeDtypeStruct(a.shape, F32)] * 2,
        in_specs=[VM] * 4,
        out_specs=[VM] * 2,
        compiler_params=params(4),
    )(a, b, c, d)


def last_kernel(scale, *refs):
    ins, out = refs[:6], refs[6]
    for side in range(2):
        a, b, c = ins[3 * side : 3 * side + 3]
        out[HALF * side : HALF * (side + 1), :] = (a[...] + b[...] + c[...]) * scale


def last_sum(scale, parts):
    return pl.pallas_call(
        lambda *refs: last_kernel(scale, *refs),
        out_shape=jax.ShapeDtypeStruct((2 * HALF, K), F32),
        in_specs=[VM] * 6,
        out_specs=VM,
        compiler_params=params(4),
    )(*parts)


def onward(value, dim):
    return lax.ppermute(value, "tm", routes(TM, dim, lambda at: 1 - 2 * (at % 2)))


def back(value, dim):
    return lax.ppermute(value, "tm", routes(TM, dim, lambda at: 2 * (at % 2) - 1))


def place_of():
    tm = lax.axis_index("tm").astype(jnp.int32)
    return tm // 8, (tm // 2) % 4, tm % 2


def unit_places(dy, dx, half):
    y, x, core = place_of()
    block = ((y + dy) % SIDE) * SIDE + (x + dx) % SIDE
    return ((block * 2 + core) * 2 + half).astype(jnp.int32), (block * 2 + half).astype(jnp.int32)


def statistics(scale, z, parts, obs_own, obs_far, load):
    _, _, core = place_of()
    every = jnp.arange(SIDE, dtype=jnp.int32)
    step, side = 1 + 2 * core, 3 - 2 * core
    a = lambda d: unit_places(every, d, 0)
    b = lambda d: unit_places(d, every, 1)
    args = (z, parts, obs_own, obs_far, load)
    far_a, far_b = stat_units([a(2), b(2)], (), *args)
    got_a, got_b = onward(far_a, X), onward(far_b, Y)
    side_a, side_b, own_a, own_b = stat_units([a(side), b(side), a(0), b(0)], (), *args)
    back_a, back_b = back(side_a, X), back(side_b, Y)
    step_a, step_b = stat_units([a(step), b(step)], (got_a, got_b), *args)
    on_a, on_b = onward(step_a, X), onward(step_b, Y)
    order = jnp.stack([0 * core + 2, side, step, 0 * core])
    far_a, side_a, step_a, own_a, far_b, side_b, step_b, own_b = join_units(
        order, (own_a, back_a, on_a, own_b, back_b, on_b)
    )
    got_a, got_b = onward(far_a, Y), onward(far_b, X)
    back_a, back_b = back(side_a, Y), back(side_b, X)
    step_a, step_b = add_two(step_a, got_a, step_b, got_b)
    on_a, on_b = onward(step_a, Y), onward(step_b, X)
    return last_sum(scale, (own_a, back_a, on_a, own_b, back_b, on_b))


def body(gains, means, transition, observations, loadings):
    tm = lax.axis_index("tm")
    zone = lax.axis_index("zone")
    zones = lax.axis_size("zone")
    y, x, core = place_of()
    one = lambda i: i.astype(jnp.int32).reshape(1)
    is_last = (tm == lax.axis_size("tm") - 1) & (zone == zones - 1)
    flip = routes(TM, CORE, lambda _: 1)

    places = jnp.concatenate([one(is_last), one(core)])
    maps, tails, shifted, whole, theirs = local_maps(places, gains, observations, means, transition)
    by_z, whole = group_maps(four_kernel, one(zone), from_later(whole, "zone", (zones,), 0))
    obs_far = lax.ppermute(theirs, "tm", flip)
    by_core, whole = group_maps(pair_kernel, one(core), from_later(whole, "tm", TM, CORE))
    by_x, whole = group_maps(four_kernel, one(x), from_later(whole, "tm", TM, X))
    parts = from_later(whole, "tm", TM, Y)
    smoothed, states = final_states(one(y), parts, by_x, by_core, by_z, tails, maps, shifted)

    both = jnp.stack([states, lax.ppermute(states, "tm", flip)])
    parts = from_later(both, "zone", (zones,), 0)
    total = lax.axis_size("tm") * zones * smoothed.shape[0]
    load_grad = statistics(1.0 / total, one(zone), parts, observations, obs_far, loadings)
    return (smoothed, load_grad)


def solution(mesh):
    return jax.shard_map(
        body,
        mesh=mesh,
        in_specs=(
            P(("tm", "zone"), None, None),
            P(("tm", "zone"), None),
            P(),
            P("tm", "zone"),
            P("zone", None),
        ),
        out_specs=(P(("tm", "zone"), None), P(("zone", "tm"), None)),
        check_vma=False,
    )
```

```python
import jax
import jax.numpy as jnp
from jax import lax
from jax.experimental import pallas as pl
from jax.experimental.pallas import tpu as pltpu
from jax.sharding import PartitionSpec as P

K = 128
AUG = 136
CHUNK = 8
SIDE = 4
WIDTH = 768
FAR_MIB, SIDE_MIB, STEP_MIB, OWN_MIB = 52, 50, 48, 46
HALF = 384
TM = (4, 4, 2)
Y, X, CORE = 0, 1, 2
FULL = lax.Precision.HIGHEST
F32 = jnp.float32
BF16 = jnp.bfloat16
NT = (((1,), (1,)), ((), ()))
NN = (((1,), (0,)), ((), ()))
VM = pl.BlockSpec(memory_space=pltpu.VMEM)
SM = pl.BlockSpec(memory_space=pltpu.SMEM)
HBM = pl.BlockSpec(memory_space=pltpu.HBM)


def params(mib):
    return pltpu.CompilerParams(vmem_limit_bytes=mib << 20)


def thirds(x):
    a = x.astype(BF16)
    x = x - a.astype(F32)
    b = x.astype(BF16)
    return a, b, (x - b.astype(F32)).astype(BF16)


def dot32(a, b, dims):
    a0, a1, a2 = thirds(a)
    b0, b1, b2 = thirds(b)
    at = dims[0][1][0]

    def two(p, q):
        left, right = jnp.concatenate(p, axis=1), jnp.concatenate(q, axis=at)
        return lax.dot_general(left, right, dims, preferred_element_type=F32)

    return two((a0, a1), (b0, b0)) + (two((a0, a1), (b1, b1)) + two((a0, a2), (b2, b0)))


def place(position):
    return position // 32, position // 8 % 4, position // 4 % 2, position % 4


def first_row(row):
    at = lax.broadcasted_iota(jnp.int32, (8, K), 0)
    return jnp.where(at == 0, jnp.broadcast_to(row, (8, K)), 0.0)


def identity_map():
    at = lax.broadcasted_iota(jnp.int32, (AUG, K), 0)
    to = lax.broadcasted_iota(jnp.int32, (AUG, K), 1)
    return jnp.where(at == to, 1.0, 0.0).astype(F32)


def then(late, early):
    out = dot32(late, early[:K], NN)
    return out + jnp.concatenate([jnp.zeros((K, K), F32), early[K:]], axis=0)


def local_kernel(last, at, g, obs, rows_in, maps, tails, shifted, whole, theirs, buf, isem, osem):
    steps = g.shape[0]
    chunks = steps // CHUNK
    units = buf.shape[0]
    _, _, core, _ = place(at[0])

    def obs_in(u):
        col = pl.multiple_of((2 * u + 1 - core) * WIDTH, WIDTH)
        return pltpu.make_async_copy(obs.at[:, pl.ds(col, WIDTH)], buf.at[u], isem.at[u])

    def obs_out(u):
        return pltpu.make_async_copy(buf.at[u], theirs.at[u], osem.at[u])

    def pass_on(u):
        obs_in(u).wait()
        obs_out(u).start()

    for u in range(units):
        obs_in(u).start()

    m = rows_in[0:steps, :]
    p = lax.dot_general(m, rows_in[steps:, :], NT, precision=FULL, preferred_element_type=F32)
    sh = jnp.concatenate([jnp.zeros((1, K), F32), p[: steps - 1]], axis=0)
    shifted[...] = sh
    whole[0:steps, :] = m - sh
    enter = jnp.where(at[0] == last, 0.0, -p[steps - 1 : steps])

    top = CHUNK - 1
    for c in range(chunks):
        t = CHUNK * c + top
        gain = g[t]
        maps[t, 0:K, :] = gain.T
        row = first_row(whole[t : t + 1, :])
        if c == chunks - 1:
            row = row + dot32(first_row(enter), gain, NT)
        maps[t, K:AUG, :] = row

    def step(i, _):
        s = top - 1 - i
        late = [maps[CHUNK * c + s + 1] for c in range(chunks)]
        gain = [g[CHUNK * c + s] for c in range(chunks)]
        out = [dot32(late[c], gain[c], NT) for c in range(chunks)]
        rows = [first_row(whole[pl.ds(CHUNK * c + s, 1), :]) for c in range(chunks)]
        for c in range(chunks):
            maps[CHUNK * c + s, 0:K, :] = out[c][:K]
            maps[CHUNK * c + s, K:AUG, :] = out[c][K:] + rows[c]
        pass_on(2 * i)
        pass_on(2 * i + 1)
        return 0

    lax.fori_loop(0, top, step, 0)
    for u in range(2 * top, units):
        pass_on(u)
    run = maps[CHUNK * (chunks - 1)]
    tails[chunks - 1] = run
    for c in range(chunks - 2, -1, -1):
        run = then(run, maps[CHUNK * c])
        tails[c] = run
    whole[...] = run
    for u in range(units):
        obs_out(u).wait()


def local_maps(last, at, gains, obs, means, transition):
    steps = gains.shape[0]
    chunks = steps // CHUNK
    rows, cols = obs.shape
    units = cols // (2 * WIDTH)
    return pl.pallas_call(
        lambda *refs: local_kernel(last, *refs),
        out_shape=(
            jax.ShapeDtypeStruct((steps, AUG, K), F32),
            jax.ShapeDtypeStruct((chunks, AUG, K), F32),
            jax.ShapeDtypeStruct((steps, K), F32),
            jax.ShapeDtypeStruct((AUG, K), F32),
            jax.ShapeDtypeStruct((units, rows, WIDTH), obs.dtype),
        ),
        in_specs=[SM, VM, HBM, VM],
        out_specs=(VM, VM, VM, VM, HBM),
        scratch_shapes=[
            pltpu.VMEM((units, rows, WIDTH), obs.dtype),
            pltpu.SemaphoreType.DMA((units,)),
            pltpu.SemaphoreType.DMA((units,)),
        ],
        compiler_params=params(44),
    )(at, gains, obs, jnp.concatenate([means, transition]))


def pick(refs, offset, count):
    offset = lax.rem(offset + count, count)
    out = refs[0][...]
    for i in range(1, count):
        out = jnp.where(offset == i, refs[i][...], out)
    return out


def four_kernel(dim, at, *refs):
    ins, (after, total) = refs[:SIDE], refs[SIDE:]
    mine = place(at[0])[dim]
    w = [pick(ins, other - mine, SIDE) for other in range(SIDE)]
    late, early = then(w[3], w[2]), then(w[1], w[0])
    total[...] = then(late, early)
    middle = then(late, w[1])
    tail = jnp.where(mine == 3, identity_map(), w[3])
    tail = jnp.where(mine == 1, late, tail)
    after[...] = jnp.where(mine == 0, middle, tail)


def pair_kernel(dim, at, mine, theirs, after, total):
    first = place(at[0])[dim] == 0
    late = jnp.where(first, theirs[...], mine[...])
    early = jnp.where(first, mine[...], theirs[...])
    after[...] = jnp.where(first, late, identity_map())
    total[...] = then(late, early)


def group_maps(kernel, dim, at, parts):
    one = jax.ShapeDtypeStruct((AUG, K), F32)
    return pl.pallas_call(
        lambda *refs: kernel(dim, *refs),
        out_shape=(one, one),
        in_specs=[SM] + [VM] * len(parts),
        out_specs=(VM, VM),
        compiler_params=params(4),
    )(at, *parts)


def apply_map(row, m):
    col = jnp.broadcast_to(row, (K, K)).T
    return jnp.sum(col * m[:K], axis=0, keepdims=True) + m[K : K + 1]


def final_kernel(at, *refs):
    ins = refs[:SIDE]
    by_x, by_core, by_z, tails, maps, shifted, smoothed, states = refs[SIDE:]
    steps = maps.shape[0]
    chunks = steps // CHUNK
    mine = place(at[0])[Y]
    v = jnp.zeros((1, K), F32)
    for other in range(SIDE - 1, 0, -1):
        v = jnp.where(other > mine, apply_map(v, pick(ins, other - mine, SIDE)), v)
    v = apply_map(v, by_x[...])
    v = apply_map(v, by_core[...])
    v = apply_map(v, by_z[...])
    col = jnp.broadcast_to(v, (K, K)).T
    for c in range(chunks):
        if c == chunks - 1:
            enter = col
        else:
            m = tails[c + 1]
            enter = jnp.sum(col * m[:K], axis=0, keepdims=True) + m[K : K + 1]
            enter = jnp.broadcast_to(enter, (K, K)).T
        rows = []
        for s in range(CHUNK):
            t = CHUNK * c + s
            rows.append(jnp.sum(enter * maps[t, 0:K, :], axis=0, keepdims=True) + maps[t, K : K + 1, :])
        out = jnp.concatenate(rows, axis=0) + shifted[CHUNK * c : CHUNK * (c + 1), :]
        smoothed[CHUNK * c : CHUNK * (c + 1), :] = out
    states[...] = smoothed[...].astype(BF16)


def final_states(at, parts, by_x, by_core, by_z, tails, maps, shifted):
    shape = shifted.shape
    return pl.pallas_call(
        final_kernel,
        out_shape=(jax.ShapeDtypeStruct(shape, F32), jax.ShapeDtypeStruct(shape, BF16)),
        in_specs=[SM] + [VM] * (SIDE + 6),
        out_specs=(VM, VM),
        compiler_params=params(4),
    )(at, *parts, by_x, by_core, by_z, tails, maps, shifted)


def routes(sizes, dim, hop_of):
    stride, total = 1, 1
    for s in sizes[dim + 1 :]:
        stride *= s
    for s in sizes:
        total *= s
    pairs = []
    for at in range(total):
        mine = (at // stride) % sizes[dim]
        pairs.append((at, at + ((mine + hop_of(at)) % sizes[dim] - mine) * stride))
    return pairs


def from_later(value, axis, sizes, dim):
    got = [value]
    for hop in range(1, sizes[dim]):
        got.append(lax.ppermute(value, axis, routes(sizes, dim, lambda _: -hop)))
    return got


LOW, HIGH = 0, 1


def stat_kernel(groups, adding, at, *refs):
    near, far, (obs_own, obs_far, load), refs = refs[:SIDE], refs[SIDE : 2 * SIDE], refs[2 * SIDE : 2 * SIDE + 3], refs[2 * SIDE + 3 :]
    adds, outs, (obs, rows_of, states, turned, sems) = refs[:adding], refs[adding:-5], refs[-5:]
    rows = near[0].shape[0]
    span = SIDE * rows
    y, x, core, z = place(at[0])

    def copies(i, j, offset, half):
        block = (y + jnp.where(core == 0, j, offset)) % SIDE * SIDE + (x + jnp.where(core == 0, offset, j)) % SIDE
        own = pl.multiple_of((2 * block + core) * WIDTH + half * HALF, HALF)
        return (
            pltpu.make_async_copy(obs_own.at[:, pl.ds(own, HALF)], obs.at[i, pl.ds(0, span)], sems.at[i, 0]),
            pltpu.make_async_copy(obs_far.at[block, :, pl.ds(half * HALF, HALF)], obs.at[i, pl.ds(span, span)], sems.at[i, 1]),
            pltpu.make_async_copy(load.at[pl.ds(own, HALF)], rows_of.at[i], sems.at[i, 2]),
        )

    jobs = [(n * SIDE + j, j, offset, half) for n, (offset, half) in enumerate(groups) for j in range(SIDE)]
    for job in jobs:
        for copy in copies(*job):
            copy.start()
    for hop in range(SIDE):
        top = pl.multiple_of((z + hop) % SIDE * rows, rows)
        states[pl.ds(top, rows), :] = near[hop][...]
        states[pl.ds(pl.multiple_of(top + span, rows), rows), :] = far[hop][...]
    turned[...] = states[...].T

    for job in jobs:
        for copy in copies(*job):
            copy.wait()
        i, j = job[:2]
        fitted = jnp.dot(rows_of[i], turned[...], preferred_element_type=F32)
        resid = (fitted - obs[i].T.astype(F32)).astype(BF16)
        term = jnp.dot(resid, states[...], preferred_element_type=F32)
        if adding:
            term = term + adds[i // SIDE][j]
        outs[i // SIDE][j] = term


def stat_units(groups, adds, limit, at, near, far, obs_own, obs_far, load):
    n = SIDE * len(groups)
    rows = obs_own.shape[0]
    flops = n * HALF * rows * 2 * K * 4
    moved = n * HALF * (rows * 4 + K * 6)
    return pl.pallas_call(
        lambda *refs: stat_kernel(groups, len(adds), *refs),
        out_shape=[jax.ShapeDtypeStruct((SIDE, HALF, K), F32)] * len(groups),
        in_specs=[SM] + [VM] * (2 * SIDE) + [HBM] * 3 + [VM] * len(adds),
        out_specs=[VM] * len(groups),
        scratch_shapes=[
            pltpu.VMEM((n, 2 * rows, HALF), BF16),
            pltpu.VMEM((n, HALF, K), BF16),
            pltpu.VMEM((2 * rows, K), BF16),
            pltpu.VMEM((K, 2 * rows), BF16),
            pltpu.SemaphoreType.DMA((n, 3)),
        ],
        cost_estimate=pl.CostEstimate(flops=flops, bytes_accessed=moved, transcendentals=0),
        compiler_params=params(limit),
    )(at, *near, *far, obs_own, obs_far, load, *adds)


def add_kernel(up, down, low, high, up_out, down_out):
    up_out[:, :HALF, :] = up[:, :HALF, :] + low[...]
    up_out[:, HALF:, :] = up[:, HALF:, :]
    down_out[:, :HALF, :] = down[:, :HALF, :]
    down_out[:, HALF:, :] = down[:, HALF:, :] + high[...]


def add_halves(up, down, low, high):
    return pl.pallas_call(
        add_kernel,
        out_shape=[jax.ShapeDtypeStruct(up.shape, F32)] * 2,
        in_specs=[VM] * 4,
        out_specs=[VM] * 2,
        compiler_params=params(12),
    )(up, down, low, high)


def join_kernel(*refs):
    ins, (low, high, up, down, own) = refs[:6], refs[6:]

    def total(d, half):
        a, b, c = ins[3 * half : 3 * half + 3]
        return a[d] + b[d] + c[d]

    low[0], high[0] = total(2, LOW), total(2, HIGH)
    for half in (LOW, HIGH):
        part = slice(HALF * half, HALF * (half + 1))
        up[0, part, :] = total(1, half)
        down[0, part, :] = total(3, half)
        own[part, :] = total(0, half)


def join_units(*parts):
    half, unit = jax.ShapeDtypeStruct((1, HALF, K), F32), jax.ShapeDtypeStruct((1, WIDTH, K), F32)
    return pl.pallas_call(
        join_kernel,
        out_shape=[half, half, unit, unit, jax.ShapeDtypeStruct((WIDTH, K), F32)],
        in_specs=[VM] * 6,
        out_specs=[VM] * 5,
        compiler_params=params(12),
    )(*parts)


def last_kernel(scale, a, b, c, out):
    out[...] = (a[...] + b[0] + c[0]) * scale


def last_sum(scale, a, b, c):
    return pl.pallas_call(
        lambda *refs: last_kernel(scale, *refs),
        out_shape=jax.ShapeDtypeStruct(a.shape, F32),
        in_specs=[VM] * 3,
        out_specs=VM,
        compiler_params=params(12),
    )(a, b, c)


def send(value, hop, first):
    pairs = [routes(TM, dim, lambda _: hop) for dim in (first, X + Y - first)]
    return lax.ppermute(value, "tm", [pairs[at % 2][at] for at in range(len(pairs[0]))])


def statistics(scale, at, near, far, obs_own, obs_far, load):
    args = (near, far, obs_own, obs_far, load)
    low, high = stat_units([(2, LOW), (2, HIGH)], (), FAR_MIB, at, *args)
    got_low, got_high = send(low, 1, X), send(high, -1, X)
    at, low, high = lax.optimization_barrier((at, low, high))
    up_high, down_low = stat_units([(1, HIGH), (3, LOW)], (), SIDE_MIB, at, *args)
    got_up_high, got_down_low = send(up_high, 1, X), send(down_low, -1, X)
    at, up_high, down_low = lax.optimization_barrier((at, up_high, down_low))
    up_low, down_high = stat_units([(1, LOW), (3, HIGH)], (got_low, got_high), STEP_MIB, at, *args)
    got_up_low, got_down_high = send(up_low, 1, X), send(down_high, -1, X)
    at, up_low, down_high = lax.optimization_barrier((at, up_low, down_high))
    own_low, own_high = stat_units([(0, LOW), (0, HIGH)], (), OWN_MIB, at, *args)
    low, high, up, down, own = join_units(own_low, got_up_low, got_down_low, own_high, got_up_high, got_down_high)
    low, high = send(low, 1, Y), send(high, -1, Y)
    up, down = add_halves(up, down, low, high)
    return last_sum(scale, own, send(up, 1, Y), send(down, -1, Y))


def body(gains, means, transition, observations, loadings):
    zones, times = lax.axis_size("zone"), lax.axis_size("tm")
    flip = routes(TM, CORE, lambda _: 1)
    swap = lambda value: lax.ppermute(value, "tm", flip)
    at = lax.axis_index(("tm", "zone")).astype(jnp.int32).reshape(1)
    maps, tails, shifted, whole, theirs = local_maps(times * zones - 1, at, gains, observations, means, transition)
    by_z, whole = group_maps(four_kernel, 3, at, from_later(whole, "zone", (zones,), 0))
    obs_far = swap(theirs)
    by_core, whole = group_maps(pair_kernel, CORE, at, from_later(whole, "tm", TM, CORE))
    by_x, whole = group_maps(four_kernel, X, at, from_later(whole, "tm", TM, X))
    whole, obs_far = lax.optimization_barrier((whole, obs_far))
    parts = from_later(whole, "tm", TM, Y)
    smoothed, states = final_states(at, parts, by_x, by_core, by_z, tails, maps, shifted)

    near = from_later(states, "zone", (zones,), 0)
    far = [swap(part) for part in near]
    total = times * zones * smoothed.shape[0]
    load_grad = statistics(1.0 / total, at, near, far, observations, obs_far, loadings)
    return (smoothed, load_grad)


def solution(mesh):
    return jax.shard_map(
        body,
        mesh=mesh,
        in_specs=(
            P(("tm", "zone"), None, None),
            P(("tm", "zone"), None),
            P(),
            P("tm", "zone"),
            P("zone", None),
        ),
        out_specs=(P(("tm", "zone"), None), P(("zone", "tm"), None)),
        check_vma=False,
    )
```

```python
import jax
import jax.numpy as jnp
from jax import lax
from jax.experimental import pallas as pl
from jax.experimental.pallas import tpu as pltpu
from jax.sharding import PartitionSpec as P

K = 128
AUG = 136
CHUNK = 8
SIDE = 4
WIDTH = 768
FAR_MIB, SIDE_MIB, STEP_MIB, OWN_MIB = 52, 50, 48, 46
HALF = 384
TM = (4, 4, 2)
Y, X, CORE = 0, 1, 2
FULL = lax.Precision.HIGHEST
F32 = jnp.float32
BF16 = jnp.bfloat16
NT = (((1,), (1,)), ((), ()))
NN = (((1,), (0,)), ((), ()))
VM = pl.BlockSpec(memory_space=pltpu.VMEM)
SM = pl.BlockSpec(memory_space=pltpu.SMEM)
HBM = pl.BlockSpec(memory_space=pltpu.HBM)


def params(mib):
    return pltpu.CompilerParams(vmem_limit_bytes=mib << 20)


def thirds(x):
    a = x.astype(BF16)
    x = x - a.astype(F32)
    b = x.astype(BF16)
    return a, b, (x - b.astype(F32)).astype(BF16)


def dot32(a, b, dims):
    a0, a1, a2 = thirds(a)
    b0, b1, b2 = thirds(b)
    at = dims[0][1][0]

    def two(p, q):
        left, right = jnp.concatenate(p, axis=1), jnp.concatenate(q, axis=at)
        return lax.dot_general(left, right, dims, preferred_element_type=F32)

    return two((a0, a1), (b0, b0)) + (two((a0, a1), (b1, b1)) + two((a0, a2), (b2, b0)))


def place(position):
    return position // 32, position // 8 % 4, position // 4 % 2, position % 4


def first_row(row):
    at = lax.broadcasted_iota(jnp.int32, (8, K), 0)
    return jnp.where(at == 0, jnp.broadcast_to(row, (8, K)), 0.0)


def identity_map():
    at = lax.broadcasted_iota(jnp.int32, (AUG, K), 0)
    to = lax.broadcasted_iota(jnp.int32, (AUG, K), 1)
    return jnp.where(at == to, 1.0, 0.0).astype(F32)


def then(late, early):
    out = dot32(late, early[:K], NN)
    return out + jnp.concatenate([jnp.zeros((K, K), F32), early[K:]], axis=0)


def local_kernel(last, at, g, obs, rows_in, maps, tails, shifted, whole, theirs, buf, isem, osem):
    steps = g.shape[0]
    chunks = steps // CHUNK
    units = buf.shape[0]
    _, _, core, _ = place(at[0])

    def obs_in(u):
        col = pl.multiple_of((2 * u + 1 - core) * WIDTH, WIDTH)
        return pltpu.make_async_copy(obs.at[:, pl.ds(col, WIDTH)], buf.at[u], isem.at[u])

    def obs_out(u):
        return pltpu.make_async_copy(buf.at[u], theirs.at[u], osem.at[u])

    def pass_on(u):
        obs_in(u).wait()
        obs_out(u).start()

    for u in range(units):
        obs_in(u).start()

    m = rows_in[0:steps, :]
    p = lax.dot_general(m, rows_in[steps:, :], NT, precision=FULL, preferred_element_type=F32)
    sh = jnp.concatenate([jnp.zeros((1, K), F32), p[: steps - 1]], axis=0)
    shifted[...] = sh
    whole[0:steps, :] = m - sh
    enter = jnp.where(at[0] == last, 0.0, -p[steps - 1 : steps])

    top = CHUNK - 1
    for c in range(chunks):
        t = CHUNK * c + top
        gain = g[t]
        maps[t, 0:K, :] = gain.T
        row = first_row(whole[t : t + 1, :])
        if c == chunks - 1:
            row = row + dot32(first_row(enter), gain, NT)
        maps[t, K:AUG, :] = row

    def step(i, _):
        s = top - 1 - i
        late = [maps[CHUNK * c + s + 1] for c in range(chunks)]
        gain = [g[CHUNK * c + s] for c in range(chunks)]
        out = [dot32(late[c], gain[c], NT) for c in range(chunks)]
        rows = [first_row(whole[pl.ds(CHUNK * c + s, 1), :]) for c in range(chunks)]
        for c in range(chunks):
            maps[CHUNK * c + s, 0:K, :] = out[c][:K]
            maps[CHUNK * c + s, K:AUG, :] = out[c][K:] + rows[c]
        pass_on(2 * i)
        pass_on(2 * i + 1)
        return 0

    lax.fori_loop(0, top, step, 0)
    for u in range(2 * top, units):
        pass_on(u)
    run = maps[CHUNK * (chunks - 1)]
    tails[chunks - 1] = run
    for c in range(chunks - 2, -1, -1):
        run = then(run, maps[CHUNK * c])
        tails[c] = run
    whole[...] = run
    for u in range(units):
        obs_out(u).wait()


def local_maps(last, at, gains, obs, means, transition):
    steps = gains.shape[0]
    chunks = steps // CHUNK
    rows, cols = obs.shape
    units = cols // (2 * WIDTH)
    return pl.pallas_call(
        lambda *refs: local_kernel(last, *refs),
        out_shape=(
            jax.ShapeDtypeStruct((steps, AUG, K), F32),
            jax.ShapeDtypeStruct((chunks, AUG, K), F32),
            jax.ShapeDtypeStruct((steps, K), F32),
            jax.ShapeDtypeStruct((AUG, K), F32),
            jax.ShapeDtypeStruct((units, rows, WIDTH), obs.dtype),
        ),
        in_specs=[SM, VM, HBM, VM],
        out_specs=(VM, VM, VM, VM, HBM),
        scratch_shapes=[
            pltpu.VMEM((units, rows, WIDTH), obs.dtype),
            pltpu.SemaphoreType.DMA((units,)),
            pltpu.SemaphoreType.DMA((units,)),
        ],
        compiler_params=params(44),
    )(at, gains, obs, jnp.concatenate([means, transition]))


def pick(refs, offset, count):
    offset = lax.rem(offset + count, count)
    out = refs[0][...]
    for i in range(1, count):
        out = jnp.where(offset == i, refs[i][...], out)
    return out


def four_kernel(dim, at, *refs):
    ins, (after, total) = refs[:SIDE], refs[SIDE:]
    mine = place(at[0])[dim]
    w = [pick(ins, other - mine, SIDE) for other in range(SIDE)]
    late, early = then(w[3], w[2]), then(w[1], w[0])
    total[...] = then(late, early)
    middle = then(late, w[1])
    tail = jnp.where(mine == 3, identity_map(), w[3])
    tail = jnp.where(mine == 1, late, tail)
    after[...] = jnp.where(mine == 0, middle, tail)


def pair_kernel(dim, at, mine, theirs, after, total):
    first = place(at[0])[dim] == 0
    late = jnp.where(first, theirs[...], mine[...])
    early = jnp.where(first, mine[...], theirs[...])
    after[...] = jnp.where(first, late, identity_map())
    total[...] = then(late, early)


def group_maps(kernel, dim, at, parts):
    one = jax.ShapeDtypeStruct((AUG, K), F32)
    return pl.pallas_call(
        lambda *refs: kernel(dim, *refs),
        out_shape=(one, one),
        in_specs=[SM] + [VM] * len(parts),
        out_specs=(VM, VM),
        compiler_params=params(4),
    )(at, *parts)


def apply_map(row, m):
    col = jnp.broadcast_to(row, (K, K)).T
    return jnp.sum(col * m[:K], axis=0, keepdims=True) + m[K : K + 1]


def final_kernel(at, *refs):
    ins = refs[:SIDE]
    by_x, by_core, by_z, tails, maps, shifted, smoothed, states = refs[SIDE:]
    steps = maps.shape[0]
    chunks = steps // CHUNK
    mine = place(at[0])[Y]
    v = jnp.zeros((1, K), F32)
    for other in range(SIDE - 1, 0, -1):
        v = jnp.where(other > mine, apply_map(v, pick(ins, other - mine, SIDE)), v)
    v = apply_map(v, by_x[...])
    v = apply_map(v, by_core[...])
    v = apply_map(v, by_z[...])
    col = jnp.broadcast_to(v, (K, K)).T
    for c in range(chunks):
        if c == chunks - 1:
            enter = col
        else:
            m = tails[c + 1]
            enter = jnp.sum(col * m[:K], axis=0, keepdims=True) + m[K : K + 1]
            enter = jnp.broadcast_to(enter, (K, K)).T
        rows = []
        for s in range(CHUNK):
            t = CHUNK * c + s
            rows.append(jnp.sum(enter * maps[t, 0:K, :], axis=0, keepdims=True) + maps[t, K : K + 1, :])
        out = jnp.concatenate(rows, axis=0) + shifted[CHUNK * c : CHUNK * (c + 1), :]
        smoothed[CHUNK * c : CHUNK * (c + 1), :] = out
    states[...] = smoothed[...].astype(BF16)


def final_states(at, parts, by_x, by_core, by_z, tails, maps, shifted):
    shape = shifted.shape
    return pl.pallas_call(
        final_kernel,
        out_shape=(jax.ShapeDtypeStruct(shape, F32), jax.ShapeDtypeStruct(shape, BF16)),
        in_specs=[SM] + [VM] * (SIDE + 6),
        out_specs=(VM, VM),
        compiler_params=params(4),
    )(at, *parts, by_x, by_core, by_z, tails, maps, shifted)


def routes(sizes, dim, hop_of):
    stride, total = 1, 1
    for s in sizes[dim + 1 :]:
        stride *= s
    for s in sizes:
        total *= s
    pairs = []
    for at in range(total):
        mine = (at // stride) % sizes[dim]
        pairs.append((at, at + ((mine + hop_of(at)) % sizes[dim] - mine) * stride))
    return pairs


def from_later(value, axis, sizes, dim):
    got = [value]
    for hop in range(1, sizes[dim]):
        got.append(lax.ppermute(value, axis, routes(sizes, dim, lambda _: -hop)))
    return got


LOW, HIGH = 0, 1
SPAN = 80.0
FOOT = 16


def put_coded(out, x):
    rows = x.shape[0]
    top = jnp.maximum(jnp.max(jnp.abs(x), axis=0, keepdims=True), 1e-30) * 1.0079
    top = top.astype(BF16).astype(F32)
    out[:rows, :] = jnp.exp(x * (SPAN / top)).astype(BF16)
    out[rows:, :] = jnp.broadcast_to(top, (FOOT, K)).astype(BF16)


def get_coded(coded):
    rows = coded.shape[0] - FOOT
    top = coded[rows:, :].astype(F32)[:1]
    return jnp.log(coded[:rows, :].astype(F32)) * (top * (1.0 / SPAN))


def stat_kernel(groups, adding, coded, scale, at, *refs):
    near, far, (obs_own, obs_far, load), refs = refs[:SIDE], refs[SIDE : 2 * SIDE], refs[2 * SIDE : 2 * SIDE + 3], refs[2 * SIDE + 3 :]
    adds, outs, (obs, rows_of, states, turned, sems) = refs[:adding], refs[adding:-5], refs[-5:]
    rows = near[0].shape[0]
    span = SIDE * rows
    y, x, core, z = place(at[0])

    def copies(i, j, offset, half):
        block = (y + jnp.where(core == 0, j, offset)) % SIDE * SIDE + (x + jnp.where(core == 0, offset, j)) % SIDE
        own = pl.multiple_of((2 * block + core) * WIDTH + half * HALF, HALF)
        return (
            pltpu.make_async_copy(obs_own.at[:, pl.ds(own, HALF)], obs.at[i, pl.ds(0, span)], sems.at[i, 0]),
            pltpu.make_async_copy(obs_far.at[block, :, pl.ds(half * HALF, HALF)], obs.at[i, pl.ds(span, span)], sems.at[i, 1]),
            pltpu.make_async_copy(load.at[pl.ds(own, HALF)], rows_of.at[i], sems.at[i, 2]),
        )

    jobs = [(n * SIDE + j, j, offset, half) for n, (offset, half) in enumerate(groups) for j in range(SIDE)]
    for job in jobs:
        for copy in copies(*job):
            copy.start()
    for hop in range(SIDE):
        top = pl.multiple_of((z + hop) % SIDE * rows, rows)
        states[pl.ds(top, rows), :] = near[hop][...]
        states[pl.ds(pl.multiple_of(top + span, rows), rows), :] = far[hop][...]
    turned[...] = states[...].T

    for job in jobs:
        for copy in copies(*job):
            copy.wait()
        i, j = job[:2]
        fitted = jnp.dot(rows_of[i], turned[...], preferred_element_type=F32)
        resid = (fitted - obs[i].T.astype(F32)).astype(BF16)
        term = jnp.dot(resid, states[...], preferred_element_type=F32) * scale
        if adding:
            term = term + get_coded(adds[i // SIDE].at[j])
        if coded:
            put_coded(outs[i // SIDE].at[j], term)
        else:
            outs[i // SIDE][j] = term


def stat_units(groups, adds, coded, scale, limit, at, near, far, obs_own, obs_far, load):
    n = SIDE * len(groups)
    rows = obs_own.shape[0]
    flops = n * HALF * rows * 2 * K * 4
    moved = n * HALF * (rows * 4 + K * 6)
    out = jax.ShapeDtypeStruct((SIDE, HALF + FOOT, K), BF16) if coded else jax.ShapeDtypeStruct((SIDE, HALF, K), F32)
    return pl.pallas_call(
        lambda *refs: stat_kernel(groups, len(adds), coded, scale, *refs),
        out_shape=[out] * len(groups),
        in_specs=[SM] + [VM] * (2 * SIDE) + [HBM] * 3 + [VM] * len(adds),
        out_specs=[VM] * len(groups),
        scratch_shapes=[
            pltpu.VMEM((n, 2 * rows, HALF), BF16),
            pltpu.VMEM((n, HALF, K), BF16),
            pltpu.VMEM((2 * rows, K), BF16),
            pltpu.VMEM((K, 2 * rows), BF16),
            pltpu.SemaphoreType.DMA((n, 3)),
        ],
        cost_estimate=pl.CostEstimate(flops=flops, bytes_accessed=moved, transcendentals=0),
        compiler_params=params(limit),
    )(at, *near, *far, obs_own, obs_far, load, *adds)


def join_kernel(*refs):
    ins, (two, one, three, own) = refs[:6], refs[6:]

    def total(d):
        halves = []
        for half in (LOW, HIGH):
            a, b, c = ins[3 * half : 3 * half + 3]
            halves.append(a[d] + get_coded(b.at[d]) + get_coded(c.at[d]))
        return jnp.concatenate(halves, axis=0)

    put_coded(two.at[0], total(2))
    put_coded(one.at[0], total(1))
    put_coded(three.at[0], total(3))
    own[...] = total(0)


def join_units(*parts):
    unit = jax.ShapeDtypeStruct((1, WIDTH + FOOT, K), BF16)
    return pl.pallas_call(
        join_kernel,
        out_shape=[unit, unit, unit, jax.ShapeDtypeStruct((WIDTH, K), F32)],
        in_specs=[VM] * 6,
        out_specs=[VM] * 4,
        compiler_params=params(12),
    )(*parts)


def last_kernel(own, two, one, three, out):
    out[...] = own[...] + get_coded(two.at[0]) + get_coded(one.at[0]) + get_coded(three.at[0])


def last_sum(own, *parts):
    return pl.pallas_call(
        last_kernel,
        out_shape=jax.ShapeDtypeStruct(own.shape, F32),
        in_specs=[VM] * 4,
        out_specs=VM,
        compiler_params=params(12),
    )(own, *parts)


def send(value, hop, first):
    pairs = [routes(TM, dim, lambda _: hop) for dim in (first, X + Y - first)]
    return lax.ppermute(value, "tm", [pairs[at % 2][at] for at in range(len(pairs[0]))])


def statistics(scale, at, near, far, obs_own, obs_far, load):
    args = (near, far, obs_own, obs_far, load)
    low, high = stat_units([(2, LOW), (2, HIGH)], (), True, scale, FAR_MIB, at, *args)
    got_low, got_high = send(low, 1, X), send(high, -1, X)
    at, low, high = lax.optimization_barrier((at, low, high))
    up_high, down_low = stat_units([(1, HIGH), (3, LOW)], (), True, scale, SIDE_MIB, at, *args)
    got_up_high, got_down_low = send(up_high, 1, X), send(down_low, -1, X)
    at, up_high, down_low = lax.optimization_barrier((at, up_high, down_low))
    up_low, down_high = stat_units([(1, LOW), (3, HIGH)], (got_low, got_high), True, scale, STEP_MIB, at, *args)
    got_up_low, got_down_high = send(up_low, 1, X), send(down_high, -1, X)
    at, up_low, down_high = lax.optimization_barrier((at, up_low, down_high))
    own_low, own_high = stat_units([(0, LOW), (0, HIGH)], (), False, scale, OWN_MIB, at, *args)
    two, one, three, own = join_units(own_low, got_up_low, got_down_low, own_high, got_up_high, got_down_high)
    return last_sum(own, send(two, 2, Y), send(one, 1, Y), send(three, -1, Y))


def body(gains, means, transition, observations, loadings):
    zones, times = lax.axis_size("zone"), lax.axis_size("tm")
    flip = routes(TM, CORE, lambda _: 1)
    swap = lambda value: lax.ppermute(value, "tm", flip)
    at = lax.axis_index(("tm", "zone")).astype(jnp.int32).reshape(1)
    maps, tails, shifted, whole, theirs = local_maps(times * zones - 1, at, gains, observations, means, transition)
    by_z, whole = group_maps(four_kernel, 3, at, from_later(whole, "zone", (zones,), 0))
    obs_far = swap(theirs)
    by_core, whole = group_maps(pair_kernel, CORE, at, from_later(whole, "tm", TM, CORE))
    by_x, whole = group_maps(four_kernel, X, at, from_later(whole, "tm", TM, X))
    whole, obs_far = lax.optimization_barrier((whole, obs_far))
    parts = from_later(whole, "tm", TM, Y)
    smoothed, states = final_states(at, parts, by_x, by_core, by_z, tails, maps, shifted)

    near = from_later(states, "zone", (zones,), 0)
    far = [swap(part) for part in near]
    total = times * zones * smoothed.shape[0]
    load_grad = statistics(1.0 / total, at, near, far, observations, obs_far, loadings)
    return (smoothed, load_grad)


def solution(mesh):
    return jax.shard_map(
        body,
        mesh=mesh,
        in_specs=(
            P(("tm", "zone"), None, None),
            P(("tm", "zone"), None),
            P(),
            P("tm", "zone"),
            P("zone", None),
        ),
        out_specs=(P(("tm", "zone"), None), P(("zone", "tm"), None)),
        check_vma=False,
    )
```

```python
import jax
import jax.numpy as jnp
from jax import lax
from jax.experimental import pallas as pl
from jax.experimental.pallas import tpu as pltpu
from jax.sharding import PartitionSpec as P

K = 128
AUG = 136
CHUNK = 8
SIDE = 4
WIDTH = 768
FAR_MIB, SIDE_MIB, STEP_MIB, OWN_MIB = 52, 50, 48, 46
HALF = 384
TM = (4, 4, 2)
Y, X, CORE = 0, 1, 2
FULL = lax.Precision.HIGHEST
F32 = jnp.float32
BF16 = jnp.bfloat16
NT = (((1,), (1,)), ((), ()))
NN = (((1,), (0,)), ((), ()))
VM = pl.BlockSpec(memory_space=pltpu.VMEM)
SM = pl.BlockSpec(memory_space=pltpu.SMEM)
HBM = pl.BlockSpec(memory_space=pltpu.HBM)


def params(mib):
    return pltpu.CompilerParams(vmem_limit_bytes=mib << 20)


def thirds(x):
    a = x.astype(BF16)
    x = x - a.astype(F32)
    b = x.astype(BF16)
    return a, b, (x - b.astype(F32)).astype(BF16)


def dot32(a, b, dims):
    a0, a1, a2 = thirds(a)
    b0, b1, b2 = thirds(b)
    at = dims[0][1][0]

    def two(p, q):
        left, right = jnp.concatenate(p, axis=1), jnp.concatenate(q, axis=at)
        return lax.dot_general(left, right, dims, preferred_element_type=F32)

    return two((a0, a1), (b0, b0)) + (two((a0, a1), (b1, b1)) + two((a0, a2), (b2, b0)))


def place(position):
    return position // 32, position // 8 % 4, position // 4 % 2, position % 4


def first_row(row):
    at = lax.broadcasted_iota(jnp.int32, (8, K), 0)
    return jnp.where(at == 0, jnp.broadcast_to(row, (8, K)), 0.0)


def identity_map():
    at = lax.broadcasted_iota(jnp.int32, (AUG, K), 0)
    to = lax.broadcasted_iota(jnp.int32, (AUG, K), 1)
    return jnp.where(at == to, 1.0, 0.0).astype(F32)


def then(late, early):
    out = dot32(late, early[:K], NN)
    return out + jnp.concatenate([jnp.zeros((K, K), F32), early[K:]], axis=0)


def local_kernel(last, at, g, obs, rows_in, maps, tails, shifted, whole, theirs, buf, isem, osem):
    steps = g.shape[0]
    chunks = steps // CHUNK
    units = buf.shape[0]
    _, _, core, _ = place(at[0])

    def obs_in(u):
        col = pl.multiple_of((2 * u + 1 - core) * WIDTH, WIDTH)
        return pltpu.make_async_copy(obs.at[:, pl.ds(col, WIDTH)], buf.at[u], isem.at[u])

    def obs_out(u):
        return pltpu.make_async_copy(buf.at[u], theirs.at[u], osem.at[u])

    def pass_on(u):
        obs_in(u).wait()
        obs_out(u).start()

    for u in range(units):
        obs_in(u).start()

    m = rows_in[0:steps, :]
    p = lax.dot_general(m, rows_in[steps:, :], NT, precision=FULL, preferred_element_type=F32)
    sh = jnp.concatenate([jnp.zeros((1, K), F32), p[: steps - 1]], axis=0)
    shifted[...] = sh
    whole[0:steps, :] = m - sh
    enter = jnp.where(at[0] == last, 0.0, -p[steps - 1 : steps])

    top = CHUNK - 1
    for c in range(chunks):
        t = CHUNK * c + top
        gain = g[t]
        maps[t, 0:K, :] = gain.T
        row = first_row(whole[t : t + 1, :])
        if c == chunks - 1:
            row = row + dot32(first_row(enter), gain, NT)
        maps[t, K:AUG, :] = row

    def step(i, _):
        s = top - 1 - i
        late = [maps[CHUNK * c + s + 1] for c in range(chunks)]
        gain = [g[CHUNK * c + s] for c in range(chunks)]
        out = [dot32(late[c], gain[c], NT) for c in range(chunks)]
        rows = [first_row(whole[pl.ds(CHUNK * c + s, 1), :]) for c in range(chunks)]
        for c in range(chunks):
            maps[CHUNK * c + s, 0:K, :] = out[c][:K]
            maps[CHUNK * c + s, K:AUG, :] = out[c][K:] + rows[c]
        pass_on(2 * i)
        pass_on(2 * i + 1)
        return 0

    lax.fori_loop(0, top, step, 0)
    for u in range(2 * top, units):
        pass_on(u)
    run = maps[CHUNK * (chunks - 1)]
    tails[chunks - 1] = run
    for c in range(chunks - 2, -1, -1):
        run = then(run, maps[CHUNK * c])
        tails[c] = run
    whole[...] = run
    for u in range(units):
        obs_out(u).wait()


def local_maps(last, at, gains, obs, means, transition):
    steps = gains.shape[0]
    chunks = steps // CHUNK
    rows, cols = obs.shape
    units = cols // (2 * WIDTH)
    return pl.pallas_call(
        lambda *refs: local_kernel(last, *refs),
        out_shape=(
            jax.ShapeDtypeStruct((steps, AUG, K), F32),
            jax.ShapeDtypeStruct((chunks, AUG, K), F32),
            jax.ShapeDtypeStruct((steps, K), F32),
            jax.ShapeDtypeStruct((AUG, K), F32),
            jax.ShapeDtypeStruct((units, rows, WIDTH), obs.dtype),
        ),
        in_specs=[SM, VM, HBM, VM],
        out_specs=(VM, VM, VM, VM, HBM),
        scratch_shapes=[
            pltpu.VMEM((units, rows, WIDTH), obs.dtype),
            pltpu.SemaphoreType.DMA((units,)),
            pltpu.SemaphoreType.DMA((units,)),
        ],
        compiler_params=params(44),
    )(at, gains, obs, jnp.concatenate([means, transition]))


def pick(refs, offset, count):
    offset = lax.rem(offset + count, count)
    out = refs[0][...]
    for i in range(1, count):
        out = jnp.where(offset == i, refs[i][...], out)
    return out


def four_kernel(dim, at, *refs):
    ins, (after, total) = refs[:SIDE], refs[SIDE:]
    mine = place(at[0])[dim]
    w = [pick(ins, other - mine, SIDE) for other in range(SIDE)]
    late, early = then(w[3], w[2]), then(w[1], w[0])
    total[...] = then(late, early)
    middle = then(late, w[1])
    tail = jnp.where(mine == 3, identity_map(), w[3])
    tail = jnp.where(mine == 1, late, tail)
    after[...] = jnp.where(mine == 0, middle, tail)


def pair_kernel(dim, at, mine, theirs, after, total):
    first = place(at[0])[dim] == 0
    late = jnp.where(first, theirs[...], mine[...])
    early = jnp.where(first, mine[...], theirs[...])
    after[...] = jnp.where(first, late, identity_map())
    total[...] = then(late, early)


def group_maps(kernel, dim, at, parts):
    one = jax.ShapeDtypeStruct((AUG, K), F32)
    return pl.pallas_call(
        lambda *refs: kernel(dim, *refs),
        out_shape=(one, one),
        in_specs=[SM] + [VM] * len(parts),
        out_specs=(VM, VM),
        compiler_params=params(4),
    )(at, *parts)


def apply_map(row, m):
    col = jnp.broadcast_to(row, (K, K)).T
    return jnp.sum(col * m[:K], axis=0, keepdims=True) + m[K : K + 1]


def final_kernel(at, *refs):
    ins = refs[:SIDE]
    by_x, by_core, by_z, tails, maps, shifted, smoothed, states = refs[SIDE:]
    steps = maps.shape[0]
    chunks = steps // CHUNK
    mine = place(at[0])[Y]
    v = jnp.zeros((1, K), F32)
    for other in range(SIDE - 1, 0, -1):
        v = jnp.where(other > mine, apply_map(v, pick(ins, other - mine, SIDE)), v)
    v = apply_map(v, by_x[...])
    v = apply_map(v, by_core[...])
    v = apply_map(v, by_z[...])
    col = jnp.broadcast_to(v, (K, K)).T
    for c in range(chunks):
        if c == chunks - 1:
            enter = col
        else:
            m = tails[c + 1]
            enter = jnp.sum(col * m[:K], axis=0, keepdims=True) + m[K : K + 1]
            enter = jnp.broadcast_to(enter, (K, K)).T
        rows = []
        for s in range(CHUNK):
            t = CHUNK * c + s
            rows.append(jnp.sum(enter * maps[t, 0:K, :], axis=0, keepdims=True) + maps[t, K : K + 1, :])
        out = jnp.concatenate(rows, axis=0) + shifted[CHUNK * c : CHUNK * (c + 1), :]
        smoothed[CHUNK * c : CHUNK * (c + 1), :] = out
    states[...] = smoothed[...].astype(BF16)


def final_states(at, parts, by_x, by_core, by_z, tails, maps, shifted):
    shape = shifted.shape
    return pl.pallas_call(
        final_kernel,
        out_shape=(jax.ShapeDtypeStruct(shape, F32), jax.ShapeDtypeStruct(shape, BF16)),
        in_specs=[SM] + [VM] * (SIDE + 6),
        out_specs=(VM, VM),
        compiler_params=params(4),
    )(at, *parts, by_x, by_core, by_z, tails, maps, shifted)


def routes(sizes, dim, hop_of):
    stride, total = 1, 1
    for s in sizes[dim + 1 :]:
        stride *= s
    for s in sizes:
        total *= s
    pairs = []
    for at in range(total):
        mine = (at // stride) % sizes[dim]
        pairs.append((at, at + ((mine + hop_of(at)) % sizes[dim] - mine) * stride))
    return pairs


def from_later(value, axis, sizes, dim):
    got = [value]
    for hop in range(1, sizes[dim]):
        got.append(lax.ppermute(value, axis, routes(sizes, dim, lambda _: -hop)))
    return got


LOW, HIGH = 0, 1
SPAN = 80.0
FOOT = 16


def put_coded(out, x):
    rows = x.shape[0]
    top = jnp.maximum(jnp.max(jnp.abs(x), axis=0, keepdims=True), 1e-30) * 1.0079
    top = top.astype(BF16).astype(F32)
    out[:rows, :] = jnp.exp(x * (SPAN / top)).astype(BF16)
    out[rows:, :] = jnp.broadcast_to(top, (FOOT, K)).astype(BF16)


def get_coded(coded):
    rows = coded.shape[0] - FOOT
    top = coded[rows:, :].astype(F32)[:1]
    return jnp.log(coded[:rows, :].astype(F32)) * (top * (1.0 / SPAN))


def stat_kernel(groups, adding, coded, scale, at, *refs):
    near, far, (obs_own, obs_far, load), refs = refs[:SIDE], refs[SIDE : 2 * SIDE], refs[2 * SIDE : 2 * SIDE + 3], refs[2 * SIDE + 3 :]
    adds, outs, (obs, rows_of, states, turned, sems) = refs[:adding], refs[adding:-5], refs[-5:]
    rows = near[0].shape[0]
    span = SIDE * rows
    y, x, core, z = place(at[0])

    def copies(i, j, offset, half):
        block = (y + jnp.where(core == 0, j, offset)) % SIDE * SIDE + (x + jnp.where(core == 0, offset, j)) % SIDE
        own = pl.multiple_of((2 * block + core) * WIDTH + half * HALF, HALF)
        return (
            pltpu.make_async_copy(obs_own.at[:, pl.ds(own, HALF)], obs.at[i, pl.ds(0, span)], sems.at[i, 0]),
            pltpu.make_async_copy(obs_far.at[block, :, pl.ds(half * HALF, HALF)], obs.at[i, pl.ds(span, span)], sems.at[i, 1]),
            pltpu.make_async_copy(load.at[pl.ds(own, HALF)], rows_of.at[i], sems.at[i, 2]),
        )

    jobs = [(n * SIDE + j, j, offset, half) for n, (offset, half) in enumerate(groups) for j in range(SIDE)]
    for job in jobs:
        for copy in copies(*job):
            copy.start()
    for hop in range(SIDE):
        top = pl.multiple_of((z + hop) % SIDE * rows, rows)
        states[pl.ds(top, rows), :] = near[hop][...]
        states[pl.ds(pl.multiple_of(top + span, rows), rows), :] = far[hop][...]
    turned[...] = states[...].T

    for first in range(0, len(jobs), 4):
        some = jobs[first : first + 4]
        for job in some:
            for copy in copies(*job):
                copy.wait()
        fits = [jnp.dot(rows_of[job[0]], turned[...], preferred_element_type=F32) for job in some]
        resids = [(f - obs[job[0]].T.astype(F32)).astype(BF16) for f, job in zip(fits, some)]
        terms = [jnp.dot(r, states[...], preferred_element_type=F32) * scale for r in resids]
        for (i, j, *_), term in zip(some, terms):
            if adding:
                term = term + get_coded(adds[i // SIDE].at[j])
            if coded:
                put_coded(outs[i // SIDE].at[j], term)
            else:
                outs[i // SIDE][j] = term


def stat_units(groups, adds, coded, scale, limit, at, near, far, obs_own, obs_far, load):
    n = SIDE * len(groups)
    rows = obs_own.shape[0]
    flops = n * HALF * rows * 2 * K * 4
    moved = n * HALF * (rows * 4 + K * 6)
    out = jax.ShapeDtypeStruct((SIDE, HALF + FOOT, K), BF16) if coded else jax.ShapeDtypeStruct((SIDE, HALF, K), F32)
    return pl.pallas_call(
        lambda *refs: stat_kernel(groups, len(adds), coded, scale, *refs),
        out_shape=[out] * len(groups),
        in_specs=[SM] + [VM] * (2 * SIDE) + [HBM] * 3 + [VM] * len(adds),
        out_specs=[VM] * len(groups),
        scratch_shapes=[
            pltpu.VMEM((n, 2 * rows, HALF), BF16),
            pltpu.VMEM((n, HALF, K), BF16),
            pltpu.VMEM((2 * rows, K), BF16),
            pltpu.VMEM((K, 2 * rows), BF16),
            pltpu.SemaphoreType.DMA((n, 3)),
        ],
        cost_estimate=pl.CostEstimate(flops=flops, bytes_accessed=moved, transcendentals=0),
        compiler_params=params(limit),
    )(at, *near, *far, obs_own, obs_far, load, *adds)


def join_kernel(*refs):
    ins, (two, one, three, own) = refs[:6], refs[6:]

    def total(d):
        halves = []
        for half in (LOW, HIGH):
            a, b, c = ins[3 * half : 3 * half + 3]
            halves.append(a[d] + get_coded(b.at[d]) + get_coded(c.at[d]))
        return jnp.concatenate(halves, axis=0)

    put_coded(two.at[0], total(2))
    put_coded(one.at[0], total(1))
    put_coded(three.at[0], total(3))
    own[...] = total(0)


def join_units(*parts):
    unit = jax.ShapeDtypeStruct((1, WIDTH + FOOT, K), BF16)
    return pl.pallas_call(
        join_kernel,
        out_shape=[unit, unit, unit, jax.ShapeDtypeStruct((WIDTH, K), F32)],
        in_specs=[VM] * 6,
        out_specs=[VM] * 4,
        compiler_params=params(12),
    )(*parts)


def last_kernel(own, two, one, three, out):
    out[...] = own[...] + get_coded(two.at[0]) + get_coded(one.at[0]) + get_coded(three.at[0])


def last_sum(own, *parts):
    return pl.pallas_call(
        last_kernel,
        out_shape=jax.ShapeDtypeStruct(own.shape, F32),
        in_specs=[VM] * 4,
        out_specs=VM,
        compiler_params=params(12),
    )(own, *parts)


def send(value, hop, first):
    pairs = [routes(TM, dim, lambda _: hop) for dim in (first, X + Y - first)]
    return lax.ppermute(value, "tm", [pairs[at % 2][at] for at in range(len(pairs[0]))])


def statistics(scale, at, near, far, obs_own, obs_far, load):
    args = (near, far, obs_own, obs_far, load)
    low, high = stat_units([(2, LOW), (2, HIGH)], (), True, scale, FAR_MIB, at, *args)
    got_low, got_high = send(low, 1, X), send(high, -1, X)
    at, low, high = lax.optimization_barrier((at, low, high))
    up_high, down_low = stat_units([(1, HIGH), (3, LOW)], (), True, scale, SIDE_MIB, at, *args)
    got_up_high, got_down_low = send(up_high, 1, X), send(down_low, -1, X)
    at, up_high, down_low = lax.optimization_barrier((at, up_high, down_low))
    up_low, down_high = stat_units([(1, LOW), (3, HIGH)], (got_low, got_high), True, scale, STEP_MIB, at, *args)
    got_up_low, got_down_high = send(up_low, 1, X), send(down_high, -1, X)
    at, up_low, down_high = lax.optimization_barrier((at, up_low, down_high))
    own_low, own_high = stat_units([(0, LOW), (0, HIGH)], (), False, scale, OWN_MIB, at, *args)
    two, one, three, own = join_units(own_low, got_up_low, got_down_low, own_high, got_up_high, got_down_high)
    return last_sum(own, send(two, 2, Y), send(one, 1, Y), send(three, -1, Y))


def body(gains, means, transition, observations, loadings):
    zones, times = lax.axis_size("zone"), lax.axis_size("tm")
    flip = routes(TM, CORE, lambda _: 1)
    swap = lambda value: lax.ppermute(value, "tm", flip)
    at = lax.axis_index(("tm", "zone")).astype(jnp.int32).reshape(1)
    maps, tails, shifted, whole, theirs = local_maps(times * zones - 1, at, gains, observations, means, transition)
    by_z, whole = group_maps(four_kernel, 3, at, from_later(whole, "zone", (zones,), 0))
    obs_far = swap(theirs)
    by_core, whole = group_maps(pair_kernel, CORE, at, from_later(whole, "tm", TM, CORE))
    by_x, whole = group_maps(four_kernel, X, at, from_later(whole, "tm", TM, X))
    whole, obs_far = lax.optimization_barrier((whole, obs_far))
    parts = from_later(whole, "tm", TM, Y)
    smoothed, states = final_states(at, parts, by_x, by_core, by_z, tails, maps, shifted)

    near = from_later(states, "zone", (zones,), 0)
    far = [swap(part) for part in near]
    total = times * zones * smoothed.shape[0]
    load_grad = statistics(1.0 / total, at, near, far, observations, obs_far, loadings)
    return (smoothed, load_grad)


def solution(mesh):
    return jax.shard_map(
        body,
        mesh=mesh,
        in_specs=(
            P(("tm", "zone"), None, None),
            P(("tm", "zone"), None),
            P(),
            P("tm", "zone"),
            P("zone", None),
        ),
        out_specs=(P(("tm", "zone"), None), P(("zone", "tm"), None)),
        check_vma=False,
    )
```

```python
import jax
import jax.numpy as jnp
from jax import lax
from jax.experimental import pallas as pl
from jax.experimental.pallas import tpu as pltpu
from jax.sharding import PartitionSpec as P

K = 128
AUG = 136
CHUNK = 8
SIDE = 4
WIDTH = 768
FAR_MIB, SIDE_MIB, STEP_MIB, OWN_MIB = 52, 50, 48, 46
HALF = 384
TM = (4, 4, 2)
Y, X, CORE = 0, 1, 2
FULL = lax.Precision.HIGHEST
F32 = jnp.float32
BF16 = jnp.bfloat16
NT = (((1,), (1,)), ((), ()))
NN = (((1,), (0,)), ((), ()))
VM = pl.BlockSpec(memory_space=pltpu.VMEM)
SM = pl.BlockSpec(memory_space=pltpu.SMEM)
HBM = pl.BlockSpec(memory_space=pltpu.HBM)


def params(mib):
    return pltpu.CompilerParams(vmem_limit_bytes=mib << 20)


def thirds(x):
    a = x.astype(BF16)
    x = x - a.astype(F32)
    b = x.astype(BF16)
    return a, b, (x - b.astype(F32)).astype(BF16)


def dot32(a, b, dims):
    a0, a1, a2 = thirds(a)
    b0, b1, b2 = thirds(b)
    at = dims[0][1][0]

    def two(p, q):
        left, right = jnp.concatenate(p, axis=1), jnp.concatenate(q, axis=at)
        return lax.dot_general(left, right, dims, preferred_element_type=F32)

    return two((a0, a1), (b0, b0)) + (two((a0, a1), (b1, b1)) + two((a0, a2), (b2, b0)))


def place(position):
    return position // 32, position // 8 % 4, position // 4 % 2, position % 4


def first_row(row):
    at = lax.broadcasted_iota(jnp.int32, (8, K), 0)
    return jnp.where(at == 0, jnp.broadcast_to(row, (8, K)), 0.0)


def identity_map():
    at = lax.broadcasted_iota(jnp.int32, (AUG, K), 0)
    to = lax.broadcasted_iota(jnp.int32, (AUG, K), 1)
    return jnp.where(at == to, 1.0, 0.0).astype(F32)


def then(late, early):
    out = dot32(late, early[:K], NN)
    return out + jnp.concatenate([jnp.zeros((K, K), F32), early[K:]], axis=0)


def local_kernel(last, at, g, obs, rows_in, maps, tails, shifted, whole, theirs, buf, isem, osem):
    steps = g.shape[0]
    chunks = steps // CHUNK
    units = buf.shape[0]
    _, _, core, _ = place(at[0])

    def obs_in(u):
        col = pl.multiple_of((2 * u + 1 - core) * WIDTH, WIDTH)
        return pltpu.make_async_copy(obs.at[:, pl.ds(col, WIDTH)], buf.at[u], isem.at[u])

    def obs_out(u):
        return pltpu.make_async_copy(buf.at[u], theirs.at[u], osem.at[u])

    def pass_on(u):
        obs_in(u).wait()
        obs_out(u).start()

    for u in range(units):
        obs_in(u).start()

    m = rows_in[0:steps, :]
    p = lax.dot_general(m, rows_in[steps:, :], NT, precision=FULL, preferred_element_type=F32)
    sh = jnp.concatenate([jnp.zeros((1, K), F32), p[: steps - 1]], axis=0)
    shifted[...] = sh
    whole[0:steps, :] = m - sh
    enter = jnp.where(at[0] == last, 0.0, -p[steps - 1 : steps])

    top = CHUNK - 1
    for c in range(chunks):
        t = CHUNK * c + top
        gain = g[t]
        maps[t, 0:K, :] = gain.T
        row = first_row(whole[t : t + 1, :])
        if c == chunks - 1:
            row = row + dot32(first_row(enter), gain, NT)
        maps[t, K:AUG, :] = row

    def step(i, _):
        s = top - 1 - i
        late = [maps[CHUNK * c + s + 1] for c in range(chunks)]
        gain = [g[CHUNK * c + s] for c in range(chunks)]
        out = [dot32(late[c], gain[c], NT) for c in range(chunks)]
        rows = [first_row(whole[pl.ds(CHUNK * c + s, 1), :]) for c in range(chunks)]
        for c in range(chunks):
            maps[CHUNK * c + s, 0:K, :] = out[c][:K]
            maps[CHUNK * c + s, K:AUG, :] = out[c][K:] + rows[c]
        pass_on(2 * i)
        pass_on(2 * i + 1)
        return 0

    lax.fori_loop(0, top, step, 0)
    for u in range(2 * top, units):
        pass_on(u)
    runs = {(c, c): maps[CHUNK * c] for c in range(chunks)}
    size = 1
    while size < chunks:
        for c in range(0, chunks, 2 * size):
            runs[c + 2 * size - 1, c] = then(runs[c + 2 * size - 1, c + size], runs[c + size - 1, c])
        size *= 2
    top = chunks - 1
    while size > 1:
        size //= 2
        for c in range(size, chunks - size, 2 * size):
            runs[top, c] = then(runs[top, c + size], runs[c + size - 1, c])
    for c in range(chunks):
        tails[c] = runs[top, c]
    whole[...] = runs[top, 0]
    for u in range(units):
        obs_out(u).wait()


def local_maps(last, at, gains, obs, means, transition):
    steps = gains.shape[0]
    chunks = steps // CHUNK
    rows, cols = obs.shape
    units = cols // (2 * WIDTH)
    return pl.pallas_call(
        lambda *refs: local_kernel(last, *refs),
        out_shape=(
            jax.ShapeDtypeStruct((steps, AUG, K), F32),
            jax.ShapeDtypeStruct((chunks, AUG, K), F32),
            jax.ShapeDtypeStruct((steps, K), F32),
            jax.ShapeDtypeStruct((AUG, K), F32),
            jax.ShapeDtypeStruct((units, rows, WIDTH), obs.dtype),
        ),
        in_specs=[SM, VM, HBM, VM],
        out_specs=(VM, VM, VM, VM, HBM),
        scratch_shapes=[
            pltpu.VMEM((units, rows, WIDTH), obs.dtype),
            pltpu.SemaphoreType.DMA((units,)),
            pltpu.SemaphoreType.DMA((units,)),
        ],
        compiler_params=params(44),
    )(at, gains, obs, jnp.concatenate([means, transition]))


def pick(refs, offset, count):
    offset = lax.rem(offset + count, count)
    out = refs[0][...]
    for i in range(1, count):
        out = jnp.where(offset == i, refs[i][...], out)
    return out


def four_kernel(dim, at, *refs):
    ins, (after, total) = refs[:SIDE], refs[SIDE:]
    mine = place(at[0])[dim]
    w = [pick(ins, other - mine, SIDE) for other in range(SIDE)]
    late, early = then(w[3], w[2]), then(w[1], w[0])
    total[...] = then(late, early)
    middle = then(late, w[1])
    tail = jnp.where(mine == 3, identity_map(), w[3])
    tail = jnp.where(mine == 1, late, tail)
    after[...] = jnp.where(mine == 0, middle, tail)


def pair_kernel(dim, at, mine, theirs, after, total):
    first = place(at[0])[dim] == 0
    late = jnp.where(first, theirs[...], mine[...])
    early = jnp.where(first, mine[...], theirs[...])
    after[...] = jnp.where(first, late, identity_map())
    total[...] = then(late, early)


def group_maps(kernel, dim, at, parts):
    one = jax.ShapeDtypeStruct((AUG, K), F32)
    return pl.pallas_call(
        lambda *refs: kernel(dim, *refs),
        out_shape=(one, one),
        in_specs=[SM] + [VM] * len(parts),
        out_specs=(VM, VM),
        compiler_params=params(4),
    )(at, *parts)


def apply_map(row, m):
    col = jnp.broadcast_to(row, (K, K)).T
    return jnp.sum(col * m[:K], axis=0, keepdims=True) + m[K : K + 1]


def final_kernel(at, *refs):
    ins = refs[:SIDE]
    by_x, by_core, by_z, tails, maps, shifted, smoothed, states = refs[SIDE:]
    steps = maps.shape[0]
    chunks = steps // CHUNK
    mine = place(at[0])[Y]
    v = jnp.zeros((1, K), F32)
    for other in range(SIDE - 1, 0, -1):
        v = jnp.where(other > mine, apply_map(v, pick(ins, other - mine, SIDE)), v)
    v = apply_map(v, by_x[...])
    v = apply_map(v, by_core[...])
    v = apply_map(v, by_z[...])
    col = jnp.broadcast_to(v, (K, K)).T
    for c in range(chunks):
        if c == chunks - 1:
            enter = col
        else:
            m = tails[c + 1]
            enter = jnp.sum(col * m[:K], axis=0, keepdims=True) + m[K : K + 1]
            enter = jnp.broadcast_to(enter, (K, K)).T
        rows = []
        for s in range(CHUNK):
            t = CHUNK * c + s
            rows.append(jnp.sum(enter * maps[t, 0:K, :], axis=0, keepdims=True) + maps[t, K : K + 1, :])
        out = jnp.concatenate(rows, axis=0) + shifted[CHUNK * c : CHUNK * (c + 1), :]
        smoothed[CHUNK * c : CHUNK * (c + 1), :] = out
    states[...] = smoothed[...].astype(BF16)


def final_states(at, parts, by_x, by_core, by_z, tails, maps, shifted):
    shape = shifted.shape
    return pl.pallas_call(
        final_kernel,
        out_shape=(jax.ShapeDtypeStruct(shape, F32), jax.ShapeDtypeStruct(shape, BF16)),
        in_specs=[SM] + [VM] * (SIDE + 6),
        out_specs=(VM, VM),
        compiler_params=params(4),
    )(at, *parts, by_x, by_core, by_z, tails, maps, shifted)


def routes(sizes, dim, hop_of):
    stride, total = 1, 1
    for s in sizes[dim + 1 :]:
        stride *= s
    for s in sizes:
        total *= s
    pairs = []
    for at in range(total):
        mine = (at // stride) % sizes[dim]
        pairs.append((at, at + ((mine + hop_of(at)) % sizes[dim] - mine) * stride))
    return pairs


def from_later(value, axis, sizes, dim):
    got = [value]
    for hop in range(1, sizes[dim]):
        got.append(lax.ppermute(value, axis, routes(sizes, dim, lambda _: -hop)))
    return got


LOW, HIGH = 0, 1
SPAN = 80.0
FOOT = 16


def put_coded(out, x):
    rows = x.shape[0]
    top = jnp.maximum(jnp.max(jnp.abs(x), axis=0, keepdims=True), 1e-30) * 1.0079
    top = top.astype(BF16).astype(F32)
    out[:rows, :] = jnp.exp(x * (SPAN / top)).astype(BF16)
    out[rows:, :] = jnp.broadcast_to(top, (FOOT, K)).astype(BF16)


def get_coded(coded):
    rows = coded.shape[0] - FOOT
    top = coded[rows:, :].astype(F32)[:1]
    return jnp.log(coded[:rows, :].astype(F32)) * (top * (1.0 / SPAN))


def stat_kernel(groups, known, adding, coded, scale, at, *refs):
    fresh, sides, (obs_own, obs_far, load), refs = known == 2 * SIDE, refs[:known], refs[known : known + 3], refs[known + 3 :]
    adds, outs, (obs, rows_of, sems) = refs[:adding], refs[adding:-3], refs[-3:]
    states, turned = outs[-2:] if fresh else sides
    span = obs_own.shape[0]
    rows = span // SIDE
    y, x, core, z = place(at[0])

    def copies(i, j, offset, half):
        block = (y + jnp.where(core == 0, j, offset)) % SIDE * SIDE + (x + jnp.where(core == 0, offset, j)) % SIDE
        own = pl.multiple_of((2 * block + core) * WIDTH + half * HALF, HALF)
        return (
            pltpu.make_async_copy(obs_own.at[:, pl.ds(own, HALF)], obs.at[i, pl.ds(0, span)], sems.at[i, 0]),
            pltpu.make_async_copy(obs_far.at[block, :, pl.ds(half * HALF, HALF)], obs.at[i, pl.ds(span, span)], sems.at[i, 1]),
            pltpu.make_async_copy(load.at[pl.ds(own, HALF)], rows_of.at[i], sems.at[i, 2]),
        )

    jobs = [(n * SIDE + j, j, offset, half) for n, (offset, half) in enumerate(groups) for j in range(SIDE)]
    for job in jobs:
        for copy in copies(*job):
            copy.start()
    if fresh:
        for hop in range(SIDE):
            top = pl.multiple_of((z + hop) % SIDE * rows, rows)
            states[pl.ds(top, rows), :] = sides[hop][...]
            states[pl.ds(pl.multiple_of(top + span, rows), rows), :] = sides[SIDE + hop][...]
        turned[...] = states[...].T

    for first in range(0, len(jobs), 4):
        some = jobs[first : first + 4]
        for job in some:
            for copy in copies(*job):
                copy.wait()
        fits = [jnp.dot(rows_of[job[0]], turned[...], preferred_element_type=F32) for job in some]
        resids = [(f - obs[job[0]].T.astype(F32)).astype(BF16) for f, job in zip(fits, some)]
        terms = [jnp.dot(r, states[...], preferred_element_type=F32) * scale for r in resids]
        for (i, j, *_), term in zip(some, terms):
            if adding:
                term = term + get_coded(adds[i // SIDE].at[j])
            if coded:
                put_coded(outs[i // SIDE].at[j], term)
            else:
                outs[i // SIDE][j] = term


def stat_units(groups, adds, coded, scale, limit, at, sides, obs_own, obs_far, load):
    n = SIDE * len(groups)
    rows = obs_own.shape[0]
    flops = n * HALF * rows * 2 * K * 4
    moved = n * HALF * (rows * 4 + K * 6)
    made = [jax.ShapeDtypeStruct(shape, BF16) for shape in ((2 * rows, K), (K, 2 * rows)) if len(sides) > 2]
    out = jax.ShapeDtypeStruct((SIDE, HALF + FOOT, K), BF16) if coded else jax.ShapeDtypeStruct((SIDE, HALF, K), F32)
    return pl.pallas_call(
        lambda *refs: stat_kernel(groups, len(sides), len(adds), coded, scale, *refs),
        out_shape=[out] * len(groups) + made,
        in_specs=[SM] + [VM] * len(sides) + [HBM] * 3 + [VM] * len(adds),
        out_specs=[VM] * (len(groups) + len(made)),
        scratch_shapes=[
            pltpu.VMEM((n, 2 * rows, HALF), BF16),
            pltpu.VMEM((n, HALF, K), BF16),
            pltpu.SemaphoreType.DMA((n, 3)),
        ],
        cost_estimate=pl.CostEstimate(flops=flops, bytes_accessed=moved, transcendentals=0),
        compiler_params=params(limit),
    )(at, *sides, obs_own, obs_far, load, *adds)


def join_kernel(*refs):
    ins, (two, one, three, own) = refs[:6], refs[6:]

    def total(d):
        halves = []
        for half in (LOW, HIGH):
            a, b, c = ins[3 * half : 3 * half + 3]
            halves.append(a[d] + get_coded(b.at[d]) + get_coded(c.at[d]))
        return jnp.concatenate(halves, axis=0)

    put_coded(two.at[0], total(2))
    put_coded(one.at[0], total(1))
    put_coded(three.at[0], total(3))
    own[...] = total(0)


def join_units(*parts):
    unit = jax.ShapeDtypeStruct((1, WIDTH + FOOT, K), BF16)
    return pl.pallas_call(
        join_kernel,
        out_shape=[unit, unit, unit, jax.ShapeDtypeStruct((WIDTH, K), F32)],
        in_specs=[VM] * 6,
        out_specs=[VM] * 4,
        compiler_params=params(12),
    )(*parts)


def last_kernel(own, two, one, three, out):
    out[...] = own[...] + get_coded(two.at[0]) + get_coded(one.at[0]) + get_coded(three.at[0])


def last_sum(own, *parts):
    return pl.pallas_call(
        last_kernel,
        out_shape=jax.ShapeDtypeStruct(own.shape, F32),
        in_specs=[VM] * 4,
        out_specs=VM,
        compiler_params=params(12),
    )(own, *parts)


def send(value, hop, first):
    pairs = [routes(TM, dim, lambda _: hop) for dim in (first, X + Y - first)]
    return lax.ppermute(value, "tm", [pairs[at % 2][at] for at in range(len(pairs[0]))])


def statistics(scale, at, near, far, obs_own, obs_far, load):
    load = (obs_own, obs_far, load)
    low, high, *sides = stat_units([(2, LOW), (2, HIGH)], (), True, scale, FAR_MIB, at, near + far, *load)
    args = (sides, *load)
    got_low, got_high = send(low, 1, X), send(high, -1, X)
    at, low, high = lax.optimization_barrier((at, low, high))
    up_high, down_low = stat_units([(1, HIGH), (3, LOW)], (), True, scale, SIDE_MIB, at, *args)
    got_up_high, got_down_low = send(up_high, 1, X), send(down_low, -1, X)
    at, up_high, down_low = lax.optimization_barrier((at, up_high, down_low))
    up_low, down_high = stat_units([(1, LOW), (3, HIGH)], (got_low, got_high), True, scale, STEP_MIB, at, *args)
    got_up_low, got_down_high = send(up_low, 1, X), send(down_high, -1, X)
    at, up_low, down_high = lax.optimization_barrier((at, up_low, down_high))
    own_low, own_high = stat_units([(0, LOW), (0, HIGH)], (), False, scale, OWN_MIB, at, *args)
    two, one, three, own = join_units(own_low, got_up_low, got_down_low, own_high, got_up_high, got_down_high)
    return last_sum(own, send(two, 2, Y), send(one, 1, Y), send(three, -1, Y))


def body(gains, means, transition, observations, loadings):
    zones, times = lax.axis_size("zone"), lax.axis_size("tm")
    flip = routes(TM, CORE, lambda _: 1)
    swap = lambda value: lax.ppermute(value, "tm", flip)
    at = lax.axis_index(("tm", "zone")).astype(jnp.int32).reshape(1)
    maps, tails, shifted, whole, theirs = local_maps(times * zones - 1, at, gains, observations, means, transition)
    by_z, whole = group_maps(four_kernel, 3, at, from_later(whole, "zone", (zones,), 0))
    obs_far = swap(theirs)
    by_core, whole = group_maps(pair_kernel, CORE, at, from_later(whole, "tm", TM, CORE))
    by_x, whole = group_maps(four_kernel, X, at, from_later(whole, "tm", TM, X))
    whole, obs_far = lax.optimization_barrier((whole, obs_far))
    parts = from_later(whole, "tm", TM, Y)
    smoothed, states = final_states(at, parts, by_x, by_core, by_z, tails, maps, shifted)

    near = from_later(states, "zone", (zones,), 0)
    far = [swap(part) for part in near]
    total = times * zones * smoothed.shape[0]
    load_grad = statistics(1.0 / total, at, near, far, observations, obs_far, loadings)
    return (smoothed, load_grad)


def solution(mesh):
    return jax.shard_map(
        body,
        mesh=mesh,
        in_specs=(
            P(("tm", "zone"), None, None),
            P(("tm", "zone"), None),
            P(),
            P("tm", "zone"),
            P("zone", None),
        ),
        out_specs=(P(("tm", "zone"), None), P(("zone", "tm"), None)),
        check_vma=False,
    )
```
